128 devices in a mesh: blk: 16 (over y, z_lo, core), cross: 8 (over z_hi, x).
Axes of the slice: x: 4, y: 4, z: 4 (z_hi: 2, z_lo: 2; z = z_hi * 2 + z_lo), core: 2. Of those that a mesh axis runs over, the one named last changes fastest.
Arguments:
- receiver_spectra: float32 [16384, 2, 1024], P(('blk', 'cross')), may hold values from -400 to 400
- source_spectra: float32 [16384, 2, 1024], P(('blk', 'cross')), may hold values from -400 to 400
- quality: int32 [16384], P(('blk', 'cross')), may hold values 0 or 1
- slot_order: int32 [128, 128], P(('blk', 'cross')), may hold values from 0 to 127, each once within a row
- owners: int32 [2, 16], replicated, may hold values from 0 to 7
Outputs:
- correlations: bfloat16 [2, 16, 8, 128, 128, 256], P(None, 'blk', 'cross')
The draws below stay inside these ranges and needn't reach their ends.
Inputs may be any that keep to these rules, and one draw needn't show every extreme that they name: `slot_order`: each row is a permutation of 0 to 127.
All inputs are finite; a program needn't handle non-finite values. No bound on the sum of `quality` on one device may be relied on, other than what follows from the above.
Results may differ from the reference program's by a relative error of at most 0.0056.
Values sent between devices are 32-bit elements; how exact they have to be, the bound alone decides.
No kernel may reach another device: no remote copies, remote signals or barrier semaphores. Data moves between devices by JAX's collectives and lax.ppermute only.
A program may use at most 128 MiB of HBM per device.

```python
import math
import jax
import jax.numpy as jnp
from jax import lax

F = 1024
L = 256
STEPS = 2
R = 128
P_SIZE = 128
RCV_ALL = 16384
SRC_ALL = 16384
N_BLK = 16
N_CROSS = 8


def spectra_law(key, rows):
    first, second, third = jax.random.split(key, 3)
    base = jnp.clip(jax.random.normal(first, (rows, 2, F), jnp.float32), -3.0, 3.0)
    row_scale = jnp.exp(jax.random.uniform(second, (rows, 1, 1), jnp.float32, 0.0, math.log(10.0)))
    bin_scale = jnp.exp(jax.random.uniform(third, (1, 1, F), jnp.float32, 0.0, math.log(10.0)))
    return base * row_scale * bin_scale


def draw_receiver_spectra(key, part):
    return spectra_law(jax.random.fold_in(key, 11), RCV_ALL)


def draw_source_spectra(key, part):
    return spectra_law(jax.random.fold_in(key, 23), SRC_ALL)


def touch_ends(values, key, low, top_value):
    shape = values.shape
    place = [jax.random.randint(jax.random.fold_in(key, axis), (), 0, shape[axis]) for axis in range(len(shape))]
    values = values.at[tuple(place)].set(low)
    longest = shape.index(max(shape))
    place[longest] = (place[longest] + 1) % shape[longest]
    return values.at[tuple(place)].set(top_value)


def setup_inputs(seed: int = 0) -> dict:
    arg_keys = jax.random.split(jax.random.key(seed), 6)
    receiver_spectra = draw_receiver_spectra(jax.random.fold_in(arg_keys[5], 71), 0)
    source_spectra = draw_source_spectra(jax.random.fold_in(arg_keys[5], 71), 0)
    quality = touch_ends((jax.random.randint(arg_keys[2], (RCV_ALL,), 0, 8) < 7).astype(jnp.int32), jax.random.fold_in(arg_keys[2], 1), 0, 1)
    slot_order = jax.vmap(lambda own: jax.random.permutation(own, R))(jax.random.split(arg_keys[3], (N_BLK * N_CROSS))).reshape((N_BLK * N_CROSS, R)).astype(jnp.int32)
    owners = touch_ends(jax.random.randint(arg_keys[4], (STEPS, N_BLK), 0, N_CROSS), jax.random.fold_in(arg_keys[4], 1), 0, N_CROSS - 1).astype(jnp.int32)
    return {"receiver_spectra": receiver_spectra, "source_spectra": source_spectra, "quality": quality, "slot_order": slot_order, "owners": owners}


def lag_tables(bins, lags):
    bin_index = jnp.arange(bins, dtype=jnp.int32)
    odd_index = 2 * jnp.arange(lags // 2, dtype=jnp.int32) + 1
    phase_turns = jnp.mod(bin_index[:, None] * odd_index[None, :], 4 * bins).astype(jnp.float32)
    phase_angle = phase_turns * (math.pi / (2 * bins))
    cos_table = (jnp.cos(phase_angle) / bins).astype(jnp.bfloat16)
    sin_table = (-jnp.sin(phase_angle) / bins).astype(jnp.bfloat16)
    return (cos_table, sin_table)

def whiten(spectra):
    mean_power = lax.optimization_barrier(jnp.mean(spectra * spectra, axis=(1, 2), keepdims=True))
    return spectra * lax.rsqrt(mean_power + 1e-06)

def correlate(panel_spec, slab_spec, cos_table, sin_table):
    npanel = panel_spec.shape[0]
    nslab = slab_spec.shape[0]
    width = math.gcd(npanel, 16)
    blocks = panel_spec.reshape(npanel // width, width, 2, panel_spec.shape[2])

    def one_block(source):
        inphase = source[:, None, 0, :] * slab_spec[None, :, 0, :] + source[:, None, 1, :] * slab_spec[None, :, 1, :]
        quadrature = source[:, None, 1, :] * slab_spec[None, :, 0, :] - source[:, None, 0, :] * slab_spec[None, :, 1, :]
        inphase = inphase.astype(jnp.bfloat16).reshape(width * nslab, -1)
        quadrature = quadrature.astype(jnp.bfloat16).reshape(width * nslab, -1)
        even = jnp.dot(inphase, cos_table, preferred_element_type=jnp.float32)
        odd = jnp.dot(quadrature, sin_table, preferred_element_type=jnp.float32)
        joined = jnp.concatenate([even + odd, even - odd], axis=-1).astype(jnp.bfloat16)
        return joined.reshape(width, nslab, -1)
    lagged = lax.map(one_block, blocks)
    return lagged.reshape(npanel, nslab, lagged.shape[-1])

def reference(receiver_spectra, source_spectra, quality, slot_order, owners):
    cos_table, sin_table = lag_tables(F, L)
    groups = N_BLK * N_CROSS
    kept = quality.astype(jnp.float32)[:, None, None]
    receivers = (whiten(receiver_spectra) * kept).reshape(groups, R, 2, F)
    receivers = jax.vmap(lambda slab_spec, order: slab_spec[order])(receivers, slot_order.reshape(groups, R))
    blocks = receivers.reshape(N_BLK, N_CROSS, R, 2, F)
    sources = whiten(source_spectra).reshape(N_BLK, N_CROSS, P_SIZE, 2, F)
    results = []
    for loop_step in range(STEPS):
        moved = jnp.roll(blocks, loop_step, axis=0).reshape(groups, R, 2, F)
        chosen = jax.vmap(lambda panels, owner: panels[owner])(sources, owners[loop_step])
        chosen = jnp.broadcast_to(chosen[:, None], (N_BLK, N_CROSS, P_SIZE, 2, F)).reshape(groups, P_SIZE, 2, F)
        lagged = lax.map(lambda pair: correlate(pair[0], pair[1], cos_table, sin_table), (chosen, moved))
        results.append(lagged.reshape(N_BLK, N_CROSS, P_SIZE, R, L))
    return jnp.stack(results)
```

```python
import functools
import math

import jax
import jax.numpy as jnp
from jax import lax
from jax.experimental import pallas as pl
from jax.experimental.pallas import tpu as pltpu
from jax.sharding import PartitionSpec as P

L = 256
STEPS = 2
F32 = jnp.float32
BF16 = jnp.bfloat16
VMEM = pl.BlockSpec(memory_space=pltpu.VMEM)
VMEM_BYTES = 56 << 20


def passed_along(value, axis, steps):
    count = lax.axis_size(axis)
    pairs = [(source, (source + steps) % count) for source in range(count)]
    return lax.ppermute(value, axis, pairs)


def lag_tables(bins, lags):
    bin_index = jnp.arange(bins, dtype=jnp.int32)
    odd_index = 2 * jnp.arange(lags // 2, dtype=jnp.int32) + 1
    phase_turns = jnp.mod(bin_index[:, None] * odd_index[None, :], 4 * bins).astype(F32)
    phase_angle = phase_turns * (math.pi / (2 * bins))
    cos_table = (jnp.cos(phase_angle) / bins).astype(BF16)
    sin_table = (-jnp.sin(phase_angle) / bins).astype(BF16)
    return (cos_table, sin_table)


def prepare_kernel(order_ref, quality_ref, raw_ref, out_ref):
    slots, _, bins = raw_ref.shape

    def eight(step, _):
        base = pl.multiple_of(step * 8, 8)
        real, imag, kept = [], [], []
        for i in range(8):
            channel = order_ref[0, base + i]
            pair = raw_ref[channel]
            real.append(pair[0:1, :])
            imag.append(pair[1:2, :])
            kept.append(jnp.full((1, 1), quality_ref[channel].astype(F32), F32))
        real = jnp.concatenate(real, axis=0)
        imag = jnp.concatenate(imag, axis=0)
        kept = jnp.concatenate(kept, axis=0)
        power = jnp.sum(real * real + imag * imag, axis=1, keepdims=True) / (2 * bins)
        scale = lax.rsqrt(power + 1e-06)
        out_ref[0, pl.ds(base, 8), :] = real * scale * kept
        out_ref[1, pl.ds(base, 8), :] = imag * scale * kept
        return 0

    lax.fori_loop(0, slots // 8, eight, 0)


def prepare(raw, quality, slot_order):
    slots, _, bins = raw.shape
    return pl.pallas_call(
        prepare_kernel,
        out_shape=jax.ShapeDtypeStruct((2, slots, bins), F32),
        in_specs=[
            pl.BlockSpec(memory_space=pltpu.SMEM),
            pl.BlockSpec(memory_space=pltpu.SMEM),
            VMEM,
        ],
        out_specs=VMEM,
        name="prepare",
        cost_estimate=pl.CostEstimate(flops=5 * raw.size, bytes_accessed=8 * raw.size, transcendentals=0),
    )(slot_order, quality, raw)


def correlate_kernel(count, aliased, place_ref, *refs):
    chunks, (slab_ref, cos_ref, sin_ref) = refs[:count], refs[count : count + 3]
    out_ref, white_ref = refs[count + 3 + aliased :]
    width, _, bins = chunks[0].shape
    slots = slab_ref.shape[1]
    half = cos_ref.shape[1]
    step = pl.program_id(0)
    for i in range(count):

        @pl.when(step == i)
        def _():
            raw = chunks[i][...]
            power = jnp.sum(jnp.sum(raw * raw, axis=2, keepdims=True), axis=1, keepdims=True) / (2 * bins)
            white_ref[...] = raw * lax.rsqrt(power + 1e-06)

    slab_re, slab_im = slab_ref[0], slab_ref[1]
    inphase, quadrature = [], []
    for p in range(width):
        pair = white_ref[p]
        re, im = pair[0:1, :], pair[1:2, :]
        inphase.append((re * slab_re + im * slab_im).astype(BF16))
        quadrature.append((im * slab_re - re * slab_im).astype(BF16))
    inphase = jnp.concatenate(inphase, axis=0)
    quadrature = jnp.concatenate(quadrature, axis=0)
    even = jnp.dot(inphase, cos_ref[...], preferred_element_type=F32)
    odd = jnp.dot(quadrature, sin_ref[...], preferred_element_type=F32)
    for p in range(width):
        e = even[p * slots : (p + 1) * slots]
        o = odd[p * slots : (p + 1) * slots]
        out_ref[p, :, :half] = (e + o).astype(BF16)
        out_ref[p, :, half:] = (e - o).astype(BF16)


def correlate(out, step, chunks, places, slab, cos_table, sin_table, sources):
    count = len(chunks)
    width, _, bins = chunks[0].shape
    slots = slab.shape[1]
    half = cos_table.shape[1]
    aliased = out is not None
    args = [*chunks, slab, cos_table, sin_table] + ([out] if aliased else [])
    grid_spec = pltpu.PrefetchScalarGridSpec(
        num_scalar_prefetch=1,
        grid=(count,),
        in_specs=[VMEM] * (count + 3) + ([pl.BlockSpec(memory_space=pl.ANY)] if aliased else []),
        out_specs=pl.BlockSpec((None, width, slots, 2 * half), lambda i, place: (step, place[i], 0, 0)),
        scratch_shapes=[pltpu.VMEM((width, 2, bins), F32)],
    )
    return pl.pallas_call(
        functools.partial(correlate_kernel, count, aliased),
        out_shape=jax.ShapeDtypeStruct((STEPS, sources, slots, 2 * half), BF16),
        grid_spec=grid_spec,
        input_output_aliases={count + 4: 0} if aliased else {},
        compiler_params=pltpu.CompilerParams(vmem_limit_bytes=VMEM_BYTES),
        name="correlate",
        cost_estimate=pl.CostEstimate(
            flops=count * width * slots * bins * 4 * 2 * half,
            bytes_accessed=count * width * slots * 2 * half * 2 + 8 * slots * bins,
            transcendentals=0,
        ),
    )(jnp.stack(places).astype(jnp.int32), *args)


def local(receiver_spectra, source_spectra, quality, slot_order, owners):
    sources, _, bins = source_spectra.shape
    members = lax.axis_size("cross")
    width = sources // members
    cos_table, sin_table = lag_tables(bins, L)
    me = lax.axis_index("cross")
    my_owners = lax.dynamic_index_in_dim(owners, lax.axis_index("blk"), 1, keepdims=False)

    slab0 = prepare(receiver_spectra, quality, slot_order)
    slab1 = passed_along(slab0, "blk", 1)
    slabs = [slab0, slab1]

    shares = lax.all_to_all(source_spectra.reshape(members, width, 2, bins), "cross", 0, 0)
    own = [lax.dynamic_index_in_dim(shares, my_owners[s], 0, keepdims=False) for s in range(STEPS)]
    chunks = [[own[s]] + [passed_along(own[s], "cross", d) for d in range(1, members)] for s in range(STEPS)]
    places = [(me - d) % members for d in range(members)]

    out = None
    for s, group in [(0, [0]), (0, [1, 2, 3]), (0, [4, 5, 6, 7]), (1, [0, 1, 2, 3, 4, 5, 6, 7])]:
        out = correlate(
            out, s, [chunks[s][d] for d in group], [places[d] for d in group],
            slabs[s], cos_table, sin_table, sources,
        )
    return out[:, None, None]


def solution(mesh):
    placed = (
        P(("blk", "cross"), None, None),
        P(("blk", "cross"), None, None),
        P(("blk", "cross")),
        P(("blk", "cross"), None),
        P(),
    )
    return jax.shard_map(
        local,
        mesh=mesh,
        in_specs=placed,
        out_specs=P(None, "blk", "cross", None, None, None),
        check_vma=False,
    )
```

```python
import functools
import math

import jax
import jax.numpy as jnp
from jax import lax
from jax.experimental import pallas as pl
from jax.experimental.pallas import tpu as pltpu
from jax.sharding import PartitionSpec as P

L = 256
STEPS = 2
F32 = jnp.float32
BF16 = jnp.bfloat16
VMEM = pl.BlockSpec(memory_space=pltpu.VMEM)
VMEM_BYTES = 56 << 20


def passed_along(value, axis, steps):
    count = lax.axis_size(axis)
    pairs = [(source, (source + steps) % count) for source in range(count)]
    return lax.ppermute(value, axis, pairs)


def lag_tables(bins, lags):
    bin_index = jnp.arange(bins, dtype=jnp.int32)
    odd_index = 2 * jnp.arange(lags // 2, dtype=jnp.int32) + 1
    phase_turns = jnp.mod(bin_index[:, None] * odd_index[None, :], 4 * bins).astype(F32)
    phase_angle = phase_turns * (math.pi / (2 * bins))
    cos_table = (jnp.cos(phase_angle) / bins).astype(BF16)
    sin_table = (-jnp.sin(phase_angle) / bins).astype(BF16)
    return (cos_table, sin_table)


def prepare_kernel(order_ref, quality_ref, raw_ref, out_ref):
    slots, _, bins = raw_ref.shape

    def eight(step, _):
        base = pl.multiple_of(step * 8, 8)
        real, imag, kept = [], [], []
        for i in range(8):
            channel = order_ref[0, base + i]
            pair = raw_ref[channel]
            real.append(pair[0:1, :])
            imag.append(pair[1:2, :])
            kept.append(jnp.full((1, 1), quality_ref[channel].astype(F32), F32))
        real = jnp.concatenate(real, axis=0)
        imag = jnp.concatenate(imag, axis=0)
        kept = jnp.concatenate(kept, axis=0)
        power = jnp.sum(real * real + imag * imag, axis=1, keepdims=True) / (2 * bins)
        scale = lax.rsqrt(power + 1e-06)
        out_ref[0, pl.ds(base, 8), :] = real * scale * kept
        out_ref[1, pl.ds(base, 8), :] = imag * scale * kept
        return 0

    lax.fori_loop(0, slots // 8, eight, 0)


def prepare(raw, quality, slot_order):
    slots, _, bins = raw.shape
    return pl.pallas_call(
        prepare_kernel,
        out_shape=jax.ShapeDtypeStruct((2, slots, bins), F32),
        in_specs=[
            pl.BlockSpec(memory_space=pltpu.SMEM),
            pl.BlockSpec(memory_space=pltpu.SMEM),
            VMEM,
        ],
        out_specs=VMEM,
        name="prepare",
        cost_estimate=pl.CostEstimate(flops=5 * raw.size, bytes_accessed=8 * raw.size, transcendentals=0),
    )(slot_order, quality, raw)


def select_kernel(mine_ref, raw_ref, own_ref, copies_ref):
    raw = raw_ref[...]
    count = 2 * raw.shape[2]
    power = jnp.sum(jnp.sum(raw * raw, axis=2, keepdims=True), axis=1, keepdims=True) / count
    white = raw * lax.rsqrt(power + 1e-06)
    own_ref[...] = white
    for i in range(copies_ref.shape[0]):
        copies_ref[i] = white


def select(shares, owner):
    members = shares.shape[0]
    share = shares.shape[1:]
    zeros = (0,) * len(share)
    return pl.pallas_call(
        select_kernel,
        out_shape=(jax.ShapeDtypeStruct(share, F32), jax.ShapeDtypeStruct(shares.shape, F32)),
        grid_spec=pltpu.PrefetchScalarGridSpec(
            num_scalar_prefetch=1,
            grid=(1,),
            in_specs=[pl.BlockSpec((None,) + share, lambda i, mine: (mine[0],) + zeros)],
            out_specs=(
                pl.BlockSpec(share, lambda i, mine: zeros),
                pl.BlockSpec((members,) + share, lambda i, mine: (0,) + zeros),
            ),
        ),
        name="select",
    )(owner, shares)


def correlate_kernel(aliased, place_ref, panel_ref, slab_ref, cos_ref, sin_ref, *refs):
    out_ref = refs[aliased]
    width = panel_ref.shape[0]
    slots = slab_ref.shape[1]
    half = cos_ref.shape[1]
    slab_re, slab_im = slab_ref[0], slab_ref[1]
    inphase, quadrature = [], []
    for p in range(width):
        pair = panel_ref[p]
        re, im = pair[0:1, :], pair[1:2, :]
        inphase.append((re * slab_re + im * slab_im).astype(BF16))
        quadrature.append((im * slab_re - re * slab_im).astype(BF16))
    inphase = jnp.concatenate(inphase, axis=0)
    quadrature = jnp.concatenate(quadrature, axis=0)
    even = jnp.dot(inphase, cos_ref[...], preferred_element_type=F32)
    odd = jnp.dot(quadrature, sin_ref[...], preferred_element_type=F32)
    for p in range(width):
        e = even[p * slots : (p + 1) * slots]
        o = odd[p * slots : (p + 1) * slots]
        out_ref[p, :, :half] = (e + o).astype(BF16)
        out_ref[p, :, half:] = (e - o).astype(BF16)


def correlate(out, step, panel, me, slab, tables, sources):
    width, _, bins = panel.shape[-3:]
    slots = slab.shape[1]
    half = tables[0].shape[1]
    aliased = out is not None
    if panel.ndim == 3:
        count = 1
        place = lambda i, mine: mine[0]
        panel_spec = pl.BlockSpec((width, 2, bins), lambda i, mine: (0, 0, 0))
    else:
        count = panel.shape[0] - 1
        place = lambda i, mine: i + (i >= mine[0]).astype(jnp.int32)
        panel_spec = pl.BlockSpec((None, width, 2, bins), lambda i, mine: (place(i, mine), 0, 0, 0))
    grid_spec = pltpu.PrefetchScalarGridSpec(
        num_scalar_prefetch=1,
        grid=(count,),
        in_specs=[panel_spec, VMEM, VMEM, VMEM] + ([pl.BlockSpec(memory_space=pl.ANY)] if aliased else []),
        out_specs=pl.BlockSpec((None, width, slots, 2 * half), lambda i, mine: (step, place(i, mine), 0, 0)),
    )
    return pl.pallas_call(
        functools.partial(correlate_kernel, int(aliased)),
        out_shape=jax.ShapeDtypeStruct((STEPS, sources, slots, 2 * half), BF16),
        grid_spec=grid_spec,
        input_output_aliases={5: 0} if aliased else {},
        compiler_params=pltpu.CompilerParams(vmem_limit_bytes=VMEM_BYTES),
        name="correlate",
        cost_estimate=pl.CostEstimate(
            flops=count * width * slots * bins * 4 * 2 * half,
            bytes_accessed=count * width * slots * 2 * half * 2 + 8 * slots * bins,
            transcendentals=0,
        ),
    )(me, panel, slab, *tables, *([out] if aliased else []))


def local(receiver_spectra, source_spectra, quality, slot_order, owners):
    sources, _, bins = source_spectra.shape
    members = lax.axis_size("cross")
    width = sources // members
    me = lax.axis_index("cross").astype(jnp.int32).reshape(1)
    mine = lax.dynamic_slice_in_dim(owners, lax.axis_index("blk"), 1, 1)

    shares = lax.all_to_all(source_spectra.reshape(members, width, 2, bins), "cross", 0, 0)
    tables = lag_tables(bins, L)
    slab0 = prepare(receiver_spectra, quality, slot_order)
    shares, slab0, tables = lax.optimization_barrier((shares, slab0, tables))
    slabs = [slab0, passed_along(slab0, "blk", 1)]

    own, panels = [], []
    for s in range(STEPS):
        share, copies = select(shares, mine[s])
        own.append(share)
        panels.append(lax.all_to_all(copies, "cross", 0, 0))

    out = None
    for panel_set in (own, panels):
        for s in range(STEPS):
            out = correlate(out, s, panel_set[s], me, slabs[s], tables, sources)
    return out[:, None, None]


def solution(mesh):
    placed = (
        P(("blk", "cross"), None, None),
        P(("blk", "cross"), None, None),
        P(("blk", "cross")),
        P(("blk", "cross"), None),
        P(),
    )
    return jax.shard_map(
        local,
        mesh=mesh,
        in_specs=placed,
        out_specs=P(None, "blk", "cross", None, None, None),
        check_vma=False,
    )
```

```python
import functools
import math

import jax
import jax.numpy as jnp
from jax import lax
from jax.experimental import pallas as pl
from jax.experimental.pallas import tpu as pltpu
from jax.sharding import PartitionSpec as P

L = 256
STEPS = 2
F32 = jnp.float32
BF16 = jnp.bfloat16
VMEM = pl.BlockSpec(memory_space=pltpu.VMEM)
VMEM_BYTES = 56 << 20


def passed_along(value, axis, steps):
    count = lax.axis_size(axis)
    pairs = [(source, (source + steps) % count) for source in range(count)]
    return lax.ppermute(value, axis, pairs)


def lag_tables(bins, lags):
    bin_index = jnp.arange(bins, dtype=jnp.int32)
    odd_index = 2 * jnp.arange(lags // 2, dtype=jnp.int32) + 1
    phase_turns = jnp.mod(bin_index[:, None] * odd_index[None, :], 4 * bins).astype(F32)
    phase_angle = phase_turns * (math.pi / (2 * bins))
    cos_table = (jnp.cos(phase_angle) / bins).astype(BF16)
    sin_table = (-jnp.sin(phase_angle) / bins).astype(BF16)
    return (cos_table, sin_table)


def prepare_kernel(order_ref, quality_ref, raw_ref, out_ref):
    slots, _, bins = raw_ref.shape

    def eight(step, _):
        base = pl.multiple_of(step * 8, 8)
        real, imag, kept = [], [], []
        for i in range(8):
            channel = order_ref[0, base + i]
            pair = raw_ref[channel]
            real.append(pair[0:1, :])
            imag.append(pair[1:2, :])
            kept.append(jnp.full((1, 1), quality_ref[channel].astype(F32), F32))
        real = jnp.concatenate(real, axis=0)
        imag = jnp.concatenate(imag, axis=0)
        kept = jnp.concatenate(kept, axis=0)
        power = jnp.sum(real * real + imag * imag, axis=1, keepdims=True) / (2 * bins)
        scale = lax.rsqrt(power + 1e-06)
        out_ref[0, pl.ds(base, 8), :] = real * scale * kept
        out_ref[1, pl.ds(base, 8), :] = imag * scale * kept
        return 0

    lax.fori_loop(0, slots // 8, eight, 0)


def prepare(raw, quality, slot_order):
    slots, _, bins = raw.shape
    return pl.pallas_call(
        prepare_kernel,
        out_shape=jax.ShapeDtypeStruct((2, slots, bins), F32),
        in_specs=[
            pl.BlockSpec(memory_space=pltpu.SMEM),
            pl.BlockSpec(memory_space=pltpu.SMEM),
            VMEM,
        ],
        out_specs=VMEM,
        name="prepare",
        cost_estimate=pl.CostEstimate(flops=5 * raw.size, bytes_accessed=8 * raw.size, transcendentals=0),
    )(slot_order, quality, raw)


def select_kernel(mine_ref, raw_ref, own_ref, copies_ref):
    raw = raw_ref[...]
    count = 2 * raw.shape[2]
    power = jnp.sum(jnp.sum(raw * raw, axis=2, keepdims=True), axis=1, keepdims=True) / count
    white = raw * lax.rsqrt(power + 1e-06)
    own_ref[...] = white
    for i in range(copies_ref.shape[0]):
        copies_ref[i] = white


def select(shares, owner):
    members = shares.shape[0]
    share = shares.shape[1:]
    zeros = (0,) * len(share)
    return pl.pallas_call(
        select_kernel,
        out_shape=(jax.ShapeDtypeStruct(share, F32), jax.ShapeDtypeStruct(shares.shape, F32)),
        grid_spec=pltpu.PrefetchScalarGridSpec(
            num_scalar_prefetch=1,
            grid=(1,),
            in_specs=[pl.BlockSpec((None,) + share, lambda i, mine: (mine[0],) + zeros)],
            out_specs=(
                pl.BlockSpec(share, lambda i, mine: zeros),
                pl.BlockSpec((members,) + share, lambda i, mine: (0,) + zeros),
            ),
        ),
        name="select",
    )(owner, shares)


def correlate_kernel(aliased, place_ref, panel_ref, slab_ref, table_ref, *refs):
    out_ref = refs[aliased]
    width = panel_ref.shape[0]
    slots, bins = slab_ref.shape[1:]
    group = math.gcd(width, 8)
    slab_re, slab_im = slab_ref[0], slab_ref[1]
    for first in range(0, width, group):
        rows = []
        for p in range(first, first + group):
            pair = panel_ref[p]
            re, im = pair[0:1, :], pair[1:2, :]
            inphase = (re * slab_re + im * slab_im).astype(BF16)
            quadrature = (im * slab_re - re * slab_im).astype(BF16)
            rows.append(jnp.concatenate([inphase, quadrature], axis=1))
        sums = jnp.dot(jnp.concatenate(rows, axis=0), table_ref[...], preferred_element_type=F32)
        for p in range(group):
            out_ref[first + p] = sums[p * slots : (p + 1) * slots].astype(BF16)


def correlate(out, step, panel, me, slab, table, sources):
    width, _, bins = panel.shape[-3:]
    slots = slab.shape[1]
    lags = table.shape[1]
    aliased = out is not None
    if panel.ndim == 3:
        count = 1
        place = lambda i, mine: mine[0]
        panel_spec = pl.BlockSpec((width, 2, bins), lambda i, mine: (0, 0, 0))
    else:
        count = panel.shape[0] - 1
        place = lambda i, mine: i + (i >= mine[0]).astype(jnp.int32)
        panel_spec = pl.BlockSpec((None, width, 2, bins), lambda i, mine: (place(i, mine), 0, 0, 0))
    grid_spec = pltpu.PrefetchScalarGridSpec(
        num_scalar_prefetch=1,
        grid=(count,),
        in_specs=[panel_spec, VMEM, VMEM] + ([pl.BlockSpec(memory_space=pl.ANY)] if aliased else []),
        out_specs=pl.BlockSpec((None, width, slots, lags), lambda i, mine: (step, place(i, mine), 0, 0)),
    )
    return pl.pallas_call(
        functools.partial(correlate_kernel, int(aliased)),
        out_shape=jax.ShapeDtypeStruct((STEPS, sources, slots, lags), BF16),
        grid_spec=grid_spec,
        input_output_aliases={4: 0} if aliased else {},
        compiler_params=pltpu.CompilerParams(vmem_limit_bytes=VMEM_BYTES),
        name="correlate",
        cost_estimate=pl.CostEstimate(
            flops=count * width * slots * bins * 4 * lags,
            bytes_accessed=count * width * slots * lags * 2 + 8 * slots * bins,
            transcendentals=0,
        ),
    )(me, panel, slab, table, *([out] if aliased else []))


def local(receiver_spectra, source_spectra, quality, slot_order, owners):
    sources, _, bins = source_spectra.shape
    members = lax.axis_size("cross")
    width = sources // members
    me = lax.axis_index("cross").astype(jnp.int32).reshape(1)
    mine = lax.dynamic_slice_in_dim(owners, lax.axis_index("blk"), 1, 1)

    shares = lax.all_to_all(source_spectra.reshape(members, width, 2, bins), "cross", 0, 0)
    cos_table, sin_table = lag_tables(bins, L)
    table = jnp.concatenate(
        [jnp.concatenate([cos_table, cos_table], axis=1), jnp.concatenate([sin_table, -sin_table], axis=1)], axis=0
    )
    slab0 = prepare(receiver_spectra, quality, slot_order)
    owner0, owner1 = mine[0], mine[1]
    shares, slab0, table, me, owner0, owner1 = lax.optimization_barrier(
        (shares, slab0, table, me, owner0, owner1)
    )

    own0, copies0 = select(shares, owner0)
    own1, copies1 = select(shares, owner1)
    panel0 = lax.all_to_all(copies0, "cross", 0, 0)
    slab1 = passed_along(slab0, "blk", 1)
    panel1 = lax.all_to_all(copies1, "cross", 0, 0)

    out = correlate(None, 0, own0, me, slab0, table, sources)
    out = correlate(out, 1, own1, me, slab1, table, sources)
    out = correlate(out, 0, panel0, me, slab0, table, sources)
    out = correlate(out, 1, panel1, me, slab1, table, sources)
    return out[:, None, None]


def solution(mesh):
    placed = (
        P(("blk", "cross"), None, None),
        P(("blk", "cross"), None, None),
        P(("blk", "cross")),
        P(("blk", "cross"), None),
        P(),
    )
    return jax.shard_map(
        local,
        mesh=mesh,
        in_specs=placed,
        out_specs=P(None, "blk", "cross", None, None, None),
        check_vma=False,
    )
```

```python
import functools
import math

import jax
import jax.numpy as jnp
from jax import lax
from jax.experimental import pallas as pl
from jax.experimental.pallas import tpu as pltpu
from jax.sharding import PartitionSpec as P

L = 256
STEPS = 2
F32 = jnp.float32
BF16 = jnp.bfloat16
VMEM = pl.BlockSpec(memory_space=pltpu.VMEM)
VMEM_BYTES = 24 << 20
SMALL_VMEM_BYTES = 8 << 20


def passed_along(value, axis, steps):
    count = lax.axis_size(axis)
    pairs = [(source, (source + steps) % count) for source in range(count)]
    return lax.ppermute(value, axis, pairs)


def lag_tables(bins, lags):
    bin_index = jnp.arange(bins, dtype=jnp.int32)
    odd_index = 2 * jnp.arange(lags // 2, dtype=jnp.int32) + 1
    phase_turns = jnp.mod(bin_index[:, None] * odd_index[None, :], 4 * bins).astype(F32)
    phase_angle = phase_turns * (math.pi / (2 * bins))
    cos_table = (jnp.cos(phase_angle) / bins).astype(BF16)
    sin_table = (-jnp.sin(phase_angle) / bins).astype(BF16)
    return (cos_table, sin_table)


def prepare_kernel(order_ref, quality_ref, raw_ref, out_ref):
    slots, _, bins = raw_ref.shape

    def eight(step, _):
        base = pl.multiple_of(step * 8, 8)
        real, imag, kept = [], [], []
        for i in range(8):
            channel = order_ref[0, base + i]
            pair = raw_ref[channel]
            real.append(pair[0:1, :])
            imag.append(pair[1:2, :])
            kept.append(jnp.full((1, 1), quality_ref[channel].astype(F32), F32))
        real = jnp.concatenate(real, axis=0)
        imag = jnp.concatenate(imag, axis=0)
        kept = jnp.concatenate(kept, axis=0)
        power = jnp.sum(real * real + imag * imag, axis=1, keepdims=True) / (2 * bins)
        scale = lax.rsqrt(power + 1e-06)
        out_ref[0, pl.ds(base, 8), :] = real * scale * kept
        out_ref[1, pl.ds(base, 8), :] = imag * scale * kept
        return 0

    lax.fori_loop(0, slots // 8, eight, 0)


def prepare(raw, quality, slot_order):
    slots, _, bins = raw.shape
    return pl.pallas_call(
        prepare_kernel,
        out_shape=jax.ShapeDtypeStruct((2, slots, bins), F32),
        in_specs=[
            pl.BlockSpec(memory_space=pltpu.SMEM),
            pl.BlockSpec(memory_space=pltpu.SMEM),
            VMEM,
        ],
        out_specs=VMEM,
        name="prepare",
        cost_estimate=pl.CostEstimate(flops=5 * raw.size, bytes_accessed=8 * raw.size, transcendentals=0),
    )(slot_order, quality, raw)


def select_kernel(owners_ref, shares_ref, own_ref, raw_ref, white_ref, read_sems, write_sems):
    steps = own_ref.shape[0]
    reads = [pltpu.make_async_copy(shares_ref.at[owners_ref[s, 0]], raw_ref.at[s], read_sems.at[s]) for s in range(steps)]
    writes = [pltpu.make_async_copy(white_ref.at[s], own_ref.at[s], write_sems.at[s]) for s in range(steps)]
    for read in reads:
        read.start()
    for s in range(steps):
        reads[s].wait()
        raw = raw_ref[s]
        count = 2 * raw.shape[2]
        power = jnp.sum(jnp.sum(raw * raw, axis=2, keepdims=True), axis=1, keepdims=True) / count
        white_ref[s] = raw * lax.rsqrt(power + 1e-06)
        writes[s].start()
    for write in writes:
        write.wait()


def select(shares, owners):
    own = (owners.shape[0],) + shares.shape[1:]
    return pl.pallas_call(
        select_kernel,
        out_shape=jax.ShapeDtypeStruct(own, F32),
        in_specs=[pl.BlockSpec(memory_space=pltpu.SMEM), pl.BlockSpec(memory_space=pl.ANY)],
        out_specs=pl.BlockSpec(memory_space=pl.ANY),
        scratch_shapes=[
            pltpu.VMEM(own, F32),
            pltpu.VMEM(own, F32),
            pltpu.SemaphoreType.DMA(own[:1]),
            pltpu.SemaphoreType.DMA(own[:1]),
        ],
        compiler_params=pltpu.CompilerParams(vmem_limit_bytes=SMALL_VMEM_BYTES),
        name="select",
    )(owners, shares)


def correlate_kernel(arrays, aliased, places_ref, *refs):
    panel_refs, (slab_ref, table_ref) = refs[:arrays], refs[arrays : arrays + 2]
    out_ref, shares_ref, sems = refs[arrays + 2 + aliased :]
    width = shares_ref.shape[1]
    slots, bins = slab_ref.shape[1:]
    group = math.gcd(width, 8)
    step = pl.program_id(0)

    @pl.when(step == 0)
    def _():
        slot = 0
        for panel_ref in panel_refs:
            for row in range(panel_ref.shape[0]):
                pltpu.make_async_copy(panel_ref.at[row], shares_ref.at[slot], sems.at[slot]).start()
                slot += 1

    share_ref = shares_ref.at[step]
    pltpu.make_async_copy(panel_refs[0].at[0], share_ref, sems.at[step]).wait()
    slab_re, slab_im = slab_ref[0], slab_ref[1]
    for first in range(0, width, group):
        rows = []
        for p in range(first, first + group):
            pair = share_ref[p]
            re, im = pair[0:1, :], pair[1:2, :]
            inphase = (re * slab_re + im * slab_im).astype(BF16)
            quadrature = (im * slab_re - re * slab_im).astype(BF16)
            rows.append(jnp.concatenate([inphase, quadrature], axis=1))
        sums = jnp.dot(jnp.concatenate(rows, axis=0), table_ref[...], preferred_element_type=F32)
        for p in range(group):
            out_ref[first + p] = sums[p * slots : (p + 1) * slots].astype(BF16)


def correlate(out, step, panels, places, first, slab, table, sources):
    width, _, bins = panels[0].shape[1:]
    slots = slab.shape[1]
    lags = table.shape[1]
    arrays = len(panels)
    count = sum(panel.shape[0] for panel in panels)
    aliased = out is not None
    anywhere = pl.BlockSpec(memory_space=pl.ANY)
    grid_spec = pltpu.PrefetchScalarGridSpec(
        num_scalar_prefetch=1,
        grid=(count,),
        in_specs=[anywhere] * arrays + [VMEM, VMEM] + [anywhere] * aliased,
        out_specs=pl.BlockSpec((None, width, slots, lags), lambda i, members: (step, members[first + i], 0, 0)),
        scratch_shapes=[pltpu.VMEM((count, width, 2, bins), F32), pltpu.SemaphoreType.DMA((count,))],
    )
    return pl.pallas_call(
        functools.partial(correlate_kernel, arrays, int(aliased)),
        out_shape=jax.ShapeDtypeStruct((STEPS, sources, slots, lags), BF16),
        grid_spec=grid_spec,
        input_output_aliases={arrays + 3: 0} if aliased else {},
        compiler_params=pltpu.CompilerParams(vmem_limit_bytes=VMEM_BYTES),
        name="correlate",
        cost_estimate=pl.CostEstimate(
            flops=count * width * slots * bins * 4 * lags,
            bytes_accessed=count * width * slots * lags * 2 + 8 * slots * bins,
            transcendentals=0,
        ),
    )(places, *panels, slab, table, *([out] if aliased else []))


def local(receiver_spectra, source_spectra, quality, slot_order, owners):
    sources, _, bins = source_spectra.shape
    members = lax.axis_size("cross")
    width = sources // members
    row = members // 2
    me = lax.axis_index("cross")
    shifts = [0, 1, row - 1] + list(range(2, row - 1))
    order = jnp.arange(members, dtype=jnp.int32)
    shift = jnp.repeat(jnp.asarray(shifts, jnp.int32), 2)
    places = (me // row + order) % 2 * row + (me % row + row - shift) % row
    mine = lax.dynamic_slice_in_dim(owners, lax.axis_index("blk"), 1, 1)

    shares = lax.all_to_all(source_spectra.reshape(members, width, 2, bins), "cross", 0, 0)
    cos_table, sin_table = lag_tables(bins, L)
    table = jnp.concatenate(
        [jnp.concatenate([cos_table, cos_table], axis=1), jnp.concatenate([sin_table, -sin_table], axis=1)], axis=0
    )
    slab0 = prepare(receiver_spectra, quality, slot_order)
    shares, slab0, table, places, mine = lax.optimization_barrier((shares, slab0, table, places, mine))

    own = select(shares, mine)
    across = [(i, (i + row) % members) for i in range(members)]
    rings = [[(i, i // row * row + (i + d) % row) for i in range(members)] for d in shifts[1:]]

    other0 = lax.ppermute(own[:1], "cross", across)
    pair0 = jnp.concatenate([own[:1], other0], axis=0)
    rest0 = [lax.ppermute(pair0, "cross", ring) for ring in rings]
    other1 = lax.ppermute(own[1:], "cross", across)
    other1, sent = lax.optimization_barrier((other1, slab0))
    slab1 = passed_along(sent, "blk", 1)
    pair1 = jnp.concatenate([own[1:], other1], axis=0)

    out = correlate(None, 0, [own[:1]], places, 0, slab0, table, sources)
    out = correlate(out, 0, [other0], places, 1, slab0, table, sources)
    out, pair1 = lax.optimization_barrier((out, pair1))
    rest1 = [lax.ppermute(pair1, "cross", ring) for ring in rings]
    out = correlate(out, 0, rest0, places, 2, slab0, table, sources)
    out = correlate(out, 1, [pair1] + rest1, places, 0, slab1, table, sources)
    return out[:, None, None]


def solution(mesh):
    placed = (
        P(("blk", "cross"), None, None),
        P(("blk", "cross"), None, None),
        P(("blk", "cross")),
        P(("blk", "cross"), None),
        P(),
    )
    return jax.shard_map(
        local,
        mesh=mesh,
        in_specs=placed,
        out_specs=P(None, "blk", "cross", None, None, None),
        check_vma=False,
    )
```

```python
import functools
import math

import jax
import jax.numpy as jnp
from jax import lax
from jax.experimental import pallas as pl
from jax.experimental.pallas import tpu as pltpu
from jax.sharding import PartitionSpec as P

L = 256
STEPS = 2
F32 = jnp.float32
BF16 = jnp.bfloat16
VMEM = pl.BlockSpec(memory_space=pltpu.VMEM)
VMEM_BYTES = 40 << 20
SMALL_VMEM_BYTES = 8 << 20


def passed_along(value, axis, steps):
    count = lax.axis_size(axis)
    pairs = [(source, (source + steps) % count) for source in range(count)]
    return lax.ppermute(value, axis, pairs)


def lag_tables(bins, lags):
    bin_index = jnp.arange(bins, dtype=jnp.int32)
    odd_index = 2 * jnp.arange(lags // 2, dtype=jnp.int32) + 1
    phase_turns = jnp.mod(bin_index[:, None] * odd_index[None, :], 4 * bins).astype(F32)
    phase_angle = phase_turns * (math.pi / (2 * bins))
    cos_table = (jnp.cos(phase_angle) / bins).astype(BF16)
    sin_table = (-jnp.sin(phase_angle) / bins).astype(BF16)
    return (cos_table, sin_table)


def prepare_kernel(order_ref, quality_ref, raw_ref, out_ref):
    slots, _, bins = raw_ref.shape

    def eight(step, _):
        base = pl.multiple_of(step * 8, 8)
        real, imag, kept = [], [], []
        for i in range(8):
            channel = order_ref[0, base + i]
            pair = raw_ref[channel]
            real.append(pair[0:1, :])
            imag.append(pair[1:2, :])
            kept.append(jnp.full((1, 1), quality_ref[channel].astype(F32), F32))
        real = jnp.concatenate(real, axis=0)
        imag = jnp.concatenate(imag, axis=0)
        kept = jnp.concatenate(kept, axis=0)
        power = jnp.sum(real * real + imag * imag, axis=1, keepdims=True) / (2 * bins)
        scale = lax.rsqrt(power + 1e-06)
        out_ref[0, pl.ds(base, 8), :] = real * scale * kept
        out_ref[1, pl.ds(base, 8), :] = imag * scale * kept
        return 0

    lax.fori_loop(0, slots // 8, eight, 0)


def prepare(raw, quality, slot_order):
    slots, _, bins = raw.shape
    return pl.pallas_call(
        prepare_kernel,
        out_shape=jax.ShapeDtypeStruct((2, slots, bins), F32),
        in_specs=[
            pl.BlockSpec(memory_space=pltpu.SMEM),
            pl.BlockSpec(memory_space=pltpu.SMEM),
            VMEM,
        ],
        out_specs=VMEM,
        name="prepare",
        cost_estimate=pl.CostEstimate(flops=5 * raw.size, bytes_accessed=8 * raw.size, transcendentals=0),
    )(slot_order, quality, raw)


def select_kernel(owners_ref, shares_ref, own_ref, raw_ref, white_ref, read_sems, write_sems):
    steps = own_ref.shape[0]
    reads = [pltpu.make_async_copy(shares_ref.at[owners_ref[s, 0]], raw_ref.at[s], read_sems.at[s]) for s in range(steps)]
    writes = [pltpu.make_async_copy(white_ref.at[s], own_ref.at[s], write_sems.at[s]) for s in range(steps)]
    for read in reads:
        read.start()
    for s in range(steps):
        reads[s].wait()
        raw = raw_ref[s]
        count = 2 * raw.shape[2]
        power = jnp.sum(jnp.sum(raw * raw, axis=2, keepdims=True), axis=1, keepdims=True) / count
        white_ref[s] = raw * lax.rsqrt(power + 1e-06)
        writes[s].start()
    for write in writes:
        write.wait()


def select(shares, owners):
    own = (owners.shape[0],) + shares.shape[1:]
    return pl.pallas_call(
        select_kernel,
        out_shape=jax.ShapeDtypeStruct(own, F32),
        in_specs=[pl.BlockSpec(memory_space=pltpu.SMEM), pl.BlockSpec(memory_space=pl.ANY)],
        out_specs=pl.BlockSpec(memory_space=pl.ANY),
        scratch_shapes=[
            pltpu.VMEM(own, F32),
            pltpu.VMEM(own, F32),
            pltpu.SemaphoreType.DMA(own[:1]),
            pltpu.SemaphoreType.DMA(own[:1]),
        ],
        compiler_params=pltpu.CompilerParams(vmem_limit_bytes=SMALL_VMEM_BYTES),
        name="select",
    )(owners, shares)


def correlate_kernel(arrays, aliased, together, columns, where_ref, *refs):
    panel_refs, (slab_ref, table_ref) = refs[:arrays], refs[arrays : arrays + 2]
    out_ref, shares_ref, sems = refs[arrays + 2 + aliased :]
    width = shares_ref.shape[1]
    slots, bins = slab_ref.shape[1:]
    group = math.gcd(width, 8)
    step = pl.program_id(0)

    @pl.when(step == 0)
    def _():
        slot = 0
        for panel_ref in panel_refs:
            for row in range(panel_ref.shape[0]):
                pltpu.make_async_copy(panel_ref.at[row], shares_ref.at[slot], sems.at[slot]).start()
                slot += 1

    for i in range(together):
        slot = step * together + i
        pltpu.make_async_copy(panel_refs[0].at[0], shares_ref.at[slot], sems.at[slot]).wait()
    slab_re, slab_im = slab_ref[0], slab_ref[1]
    for i in range(together):
        share_ref = shares_ref.at[step * together + lax.rem(lax.div(where_ref[0], columns) + i, together)]
        for first in range(0, width, group):
            rows = []
            for p in range(first, first + group):
                pair = share_ref[p]
                re, im = pair[0:1, :], pair[1:2, :]
                inphase = (re * slab_re + im * slab_im).astype(BF16)
                quadrature = (im * slab_re - re * slab_im).astype(BF16)
                rows.append(jnp.concatenate([inphase, quadrature], axis=1))
            sums = jnp.dot(jnp.concatenate(rows, axis=0), table_ref[...], preferred_element_type=F32)
            for p in range(group):
                out_ref[i, first + p] = sums[p * slots : (p + 1) * slots].astype(BF16)


def correlate(out, step, panels, where, first, slab, table, columns, shifts, half=None):
    width, _, bins = panels[0].shape[1:]
    slots = slab.shape[1]
    lags = table.shape[1]
    arrays = len(panels)
    count = sum(panel.shape[0] for panel in panels)
    together = 2 if half is None else 1
    aliased = out is not None
    anywhere = pl.BlockSpec(memory_space=pl.ANY)

    def block(i, where):
        row = 0 if half is None else lax.rem(lax.div(where[0], columns) + half, 2)
        shift = sum(((i + first == a).astype(jnp.int32) * d for a, d in enumerate(shifts) if d), 0)
        return (step, row, lax.rem(where[0] + (columns - shift), columns), 0, 0, 0)

    grid_spec = pltpu.PrefetchScalarGridSpec(
        num_scalar_prefetch=1,
        grid=(count // together,),
        in_specs=[anywhere] * arrays + [VMEM, VMEM] + [anywhere] * aliased,
        out_specs=pl.BlockSpec((None, together, None, width, slots, lags), block),
        scratch_shapes=[pltpu.VMEM((count, width, 2, bins), F32), pltpu.SemaphoreType.DMA((count,))],
    )
    return pl.pallas_call(
        functools.partial(correlate_kernel, arrays, int(aliased), together, columns),
        out_shape=jax.ShapeDtypeStruct((STEPS, 2, columns, width, slots, lags), BF16),
        grid_spec=grid_spec,
        input_output_aliases={arrays + 3: 0} if aliased else {},
        compiler_params=pltpu.CompilerParams(vmem_limit_bytes=VMEM_BYTES),
        name="correlate",
        cost_estimate=pl.CostEstimate(
            flops=count * width * slots * bins * 4 * lags,
            bytes_accessed=count * width * slots * lags * 2 + 8 * slots * bins,
            transcendentals=0,
        ),
    )(where, *panels, slab, table, *([out] if aliased else []))


def local(receiver_spectra, source_spectra, quality, slot_order, owners):
    sources, _, bins = source_spectra.shape
    members = lax.axis_size("cross")
    width = sources // members
    row = members // 2
    me = lax.axis_index("cross")
    shifts = [0, 1, row - 1] + list(range(2, row - 1))
    where = me.astype(jnp.int32).reshape(1)
    mine = lax.dynamic_slice_in_dim(owners, lax.axis_index("blk"), 1, 1)

    shares = lax.all_to_all(source_spectra.reshape(members, width, 2, bins), "cross", 0, 0)
    cos_table, sin_table = lag_tables(bins, L)
    table = jnp.concatenate(
        [jnp.concatenate([cos_table, cos_table], axis=1), jnp.concatenate([sin_table, -sin_table], axis=1)], axis=0
    )
    slab0 = prepare(receiver_spectra, quality, slot_order)
    shares, slab0, table, where, mine = lax.optimization_barrier((shares, slab0, table, where, mine))

    own = select(shares, mine)
    across = [(i, (i + row) % members) for i in range(members)]
    rings = [[(i, i // row * row + (i + d) % row) for i in range(members)] for d in shifts[1:]]

    other0 = lax.ppermute(own[:1], "cross", across)
    pair0 = jnp.concatenate([own[:1], other0], axis=0)
    rest0 = [lax.ppermute(pair0, "cross", ring) for ring in rings]
    other1 = lax.ppermute(own[1:], "cross", across)
    other1, sent = lax.optimization_barrier((other1, slab0))
    slab1 = passed_along(sent, "blk", 1)
    pair1 = jnp.concatenate([own[1:], other1], axis=0)

    out = correlate(None, 0, [own[:1]], where, 0, slab0, table, row, shifts, half=0)
    out = correlate(out, 0, [other0], where, 0, slab0, table, row, shifts, half=1)
    out, pair1 = lax.optimization_barrier((out, pair1))
    rest1 = [lax.ppermute(pair1, "cross", ring) for ring in rings]
    out = correlate(out, 0, rest0, where, 1, slab0, table, row, shifts)
    out = correlate(out, 1, [pair1] + rest1, where, 0, slab1, table, row, shifts)
    slots, lags = out.shape[-2:]
    return out.reshape(STEPS, 1, 1, sources, slots, lags)


def solution(mesh):
    placed = (
        P(("blk", "cross"), None, None),
        P(("blk", "cross"), None, None),
        P(("blk", "cross")),
        P(("blk", "cross"), None),
        P(),
    )
    return jax.shard_map(
        local,
        mesh=mesh,
        in_specs=placed,
        out_specs=P(None, "blk", "cross", None, None, None),
        check_vma=False,
    )
```

```python
import functools
import math

import jax
import jax.numpy as jnp
from jax import lax
from jax.experimental import pallas as pl
from jax.experimental.pallas import tpu as pltpu
from jax.sharding import PartitionSpec as P

L = 256
STEPS = 2
F32 = jnp.float32
BF16 = jnp.bfloat16
VMEM = pl.BlockSpec(memory_space=pltpu.VMEM)
VMEM_BYTES = 40 << 20
SMALL_VMEM_BYTES = 8 << 20


def passed_along(value, axis, steps):
    count = lax.axis_size(axis)
    pairs = [(source, (source + steps) % count) for source in range(count)]
    return lax.ppermute(value, axis, pairs)


def lag_tables(bins, lags):
    bin_index = jnp.arange(bins, dtype=jnp.int32)
    odd_index = 2 * jnp.arange(lags // 2, dtype=jnp.int32) + 1
    phase_turns = jnp.mod(bin_index[:, None] * odd_index[None, :], 4 * bins).astype(F32)
    phase_angle = phase_turns * (math.pi / (2 * bins))
    cos_table = (jnp.cos(phase_angle) / bins).astype(BF16)
    sin_table = (-jnp.sin(phase_angle) / bins).astype(BF16)
    return (cos_table, sin_table)


def prepare_kernel(order_ref, quality_ref, raw_ref, out_ref):
    slots, _, bins = raw_ref.shape

    def eight(step, _):
        base = pl.multiple_of(step * 8, 8)
        real, imag, kept = [], [], []
        for i in range(8):
            channel = order_ref[0, base + i]
            pair = raw_ref[channel]
            real.append(pair[0:1, :])
            imag.append(pair[1:2, :])
            kept.append(jnp.full((1, 1), quality_ref[channel].astype(F32), F32))
        real = jnp.concatenate(real, axis=0)
        imag = jnp.concatenate(imag, axis=0)
        kept = jnp.concatenate(kept, axis=0)
        power = jnp.sum(real * real + imag * imag, axis=1, keepdims=True) / (2 * bins)
        scale = lax.rsqrt(power + 1e-06)
        out_ref[0, pl.ds(base, 8), :] = real * scale * kept
        out_ref[1, pl.ds(base, 8), :] = imag * scale * kept
        return 0

    lax.fori_loop(0, slots // 8, eight, 0)


def prepare(raw, quality, slot_order):
    slots, _, bins = raw.shape
    return pl.pallas_call(
        prepare_kernel,
        out_shape=jax.ShapeDtypeStruct((2, slots, bins), F32),
        in_specs=[
            pl.BlockSpec(memory_space=pltpu.SMEM),
            pl.BlockSpec(memory_space=pltpu.SMEM),
            VMEM,
        ],
        out_specs=VMEM,
        name="prepare",
        cost_estimate=pl.CostEstimate(flops=5 * raw.size, bytes_accessed=8 * raw.size, transcendentals=0),
    )(slot_order, quality, raw)


def select_kernel(owners_ref, shares_ref, own_ref, raw_ref, white_ref, read_sems, write_sems):
    steps = own_ref.shape[0]
    reads = [pltpu.make_async_copy(shares_ref.at[owners_ref[s, 0]], raw_ref.at[s], read_sems.at[s]) for s in range(steps)]
    writes = [pltpu.make_async_copy(white_ref.at[s], own_ref.at[s], write_sems.at[s]) for s in range(steps)]
    for read in reads:
        read.start()
    for s in range(steps):
        reads[s].wait()
        raw = raw_ref[s]
        count = 2 * raw.shape[2]
        power = jnp.sum(jnp.sum(raw * raw, axis=2, keepdims=True), axis=1, keepdims=True) / count
        white_ref[s] = raw * lax.rsqrt(power + 1e-06)
        writes[s].start()
    for write in writes:
        write.wait()


def select(shares, owners):
    own = (owners.shape[0],) + shares.shape[1:]
    return pl.pallas_call(
        select_kernel,
        out_shape=jax.ShapeDtypeStruct(own, F32),
        in_specs=[pl.BlockSpec(memory_space=pltpu.SMEM), pl.BlockSpec(memory_space=pl.ANY)],
        out_specs=pl.BlockSpec(memory_space=pl.ANY),
        scratch_shapes=[
            pltpu.VMEM(own, F32),
            pltpu.VMEM(own, F32),
            pltpu.SemaphoreType.DMA(own[:1]),
            pltpu.SemaphoreType.DMA(own[:1]),
        ],
        compiler_params=pltpu.CompilerParams(vmem_limit_bytes=SMALL_VMEM_BYTES),
        name="select",
    )(owners, shares)


def correlate_kernel(arrays, aliased, together, columns, where_ref, *refs):
    panel_refs, (slab_ref, table_ref) = refs[:arrays], refs[arrays : arrays + 2]
    out_ref, shares_ref, sems = refs[arrays + 2 + aliased :]
    width = shares_ref.shape[1]
    slots, bins = slab_ref.shape[1:]
    group = math.gcd(width, 8)
    step = pl.program_id(0)

    @pl.when(step == 0)
    def _():
        slot = 0
        for panel_ref in panel_refs:
            for row in range(panel_ref.shape[0]):
                pltpu.make_async_copy(panel_ref.at[row], shares_ref.at[slot], sems.at[slot]).start()
                slot += 1

    for i in range(together):
        slot = step * together + i
        pltpu.make_async_copy(panel_refs[0].at[0], shares_ref.at[slot], sems.at[slot]).wait()
    slab_re, slab_im = slab_ref[0], slab_ref[1]
    for i in range(together):
        share_ref = shares_ref.at[step * together + lax.rem(lax.div(where_ref[0], columns) + i, together)]
        for first in range(0, width, group):
            rows = []
            for p in range(first, first + group):
                pair = share_ref[p]
                re, im = pair[0:1, :], pair[1:2, :]
                inphase = (re * slab_re + im * slab_im).astype(BF16)
                quadrature = (im * slab_re - re * slab_im).astype(BF16)
                rows.append(jnp.concatenate([inphase, quadrature], axis=1))
            sums = jnp.dot(jnp.concatenate(rows, axis=0), table_ref[...], preferred_element_type=F32)
            for p in range(group):
                out_ref[i, first + p] = sums[p * slots : (p + 1) * slots].astype(BF16)


def correlate(out, step, panels, where, first, slab, table, columns, shifts, half=None):
    width, _, bins = panels[0].shape[1:]
    slots = slab.shape[1]
    lags = table.shape[1]
    arrays = len(panels)
    count = sum(panel.shape[0] for panel in panels)
    together = 2 if half is None else 1
    aliased = out is not None
    anywhere = pl.BlockSpec(memory_space=pl.ANY)

    def block(i, where):
        row = 0 if half is None else lax.rem(lax.div(where[0], columns) + half, 2)
        shift = sum(((i + first == a).astype(jnp.int32) * d for a, d in enumerate(shifts) if d), 0)
        return (step, row, lax.rem(where[0] + (columns - shift), columns), 0, 0, 0)

    grid_spec = pltpu.PrefetchScalarGridSpec(
        num_scalar_prefetch=1,
        grid=(count // together,),
        in_specs=[anywhere] * arrays + [VMEM, VMEM] + [anywhere] * aliased,
        out_specs=pl.BlockSpec((None, together, None, width, slots, lags), block),
        scratch_shapes=[pltpu.VMEM((count, width, 2, bins), F32), pltpu.SemaphoreType.DMA((count,))],
    )
    return pl.pallas_call(
        functools.partial(correlate_kernel, arrays, int(aliased), together, columns),
        out_shape=jax.ShapeDtypeStruct((STEPS, 2, columns, width, slots, lags), BF16),
        grid_spec=grid_spec,
        input_output_aliases={arrays + 3: 0} if aliased else {},
        compiler_params=pltpu.CompilerParams(vmem_limit_bytes=VMEM_BYTES),
        name="correlate",
        cost_estimate=pl.CostEstimate(
            flops=count * width * slots * bins * 4 * lags,
            bytes_accessed=count * width * slots * lags * 2 + 8 * slots * bins,
            transcendentals=0,
        ),
    )(where, *panels, slab, table, *([out] if aliased else []))


def local(receiver_spectra, source_spectra, quality, slot_order, owners):
    sources, _, bins = source_spectra.shape
    members = lax.axis_size("cross")
    width = sources // members
    row = members // 2
    me = lax.axis_index("cross")
    shifts = [0, 1, row - 1] + list(range(2, row - 1))
    where = me.astype(jnp.int32).reshape(1)
    mine = lax.dynamic_slice_in_dim(owners, lax.axis_index("blk"), 1, 1)

    shares = lax.all_to_all(source_spectra.reshape(members, width, 2, bins), "cross", 0, 0)
    cos_table, sin_table = lag_tables(bins, L)
    table = jnp.concatenate(
        [jnp.concatenate([cos_table, cos_table], axis=1), jnp.concatenate([sin_table, -sin_table], axis=1)], axis=0
    )
    slab0 = prepare(receiver_spectra, quality, slot_order)
    shares, slab0, table, where, mine = lax.optimization_barrier((shares, slab0, table, where, mine))

    own = select(shares, mine)
    across = [(i, (i + row) % members) for i in range(members)]
    rings = [[(i, i // row * row + (i + d) % row) for i in range(members)] for d in shifts[1:]]

    other0 = lax.ppermute(own[:1], "cross", across)
    pair0 = jnp.concatenate([own[:1], other0], axis=0)
    pair0, own1 = lax.optimization_barrier((pair0, own[1:]))
    rest0 = [lax.ppermute(pair0, "cross", ring) for ring in rings]
    other1 = lax.ppermute(own1, "cross", across)
    other1, sent = lax.optimization_barrier((other1, slab0))
    slab1 = passed_along(sent, "blk", 1)
    pair1 = jnp.concatenate([own[1:], other1], axis=0)

    out = correlate(None, 0, [own[:1]], where, 0, slab0, table, row, shifts, half=0)
    out = correlate(out, 0, [other0], where, 0, slab0, table, row, shifts, half=1)
    out, pair1 = lax.optimization_barrier((out, pair1))
    rest1 = [lax.ppermute(pair1, "cross", ring) for ring in rings]
    out = correlate(out, 0, rest0, where, 1, slab0, table, row, shifts)
    out = correlate(out, 1, [pair1] + rest1, where, 0, slab1, table, row, shifts)
    slots, lags = out.shape[-2:]
    return out.reshape(STEPS, 1, 1, sources, slots, lags)


def solution(mesh):
    placed = (
        P(("blk", "cross"), None, None),
        P(("blk", "cross"), None, None),
        P(("blk", "cross")),
        P(("blk", "cross"), None),
        P(),
    )
    return jax.shard_map(
        local,
        mesh=mesh,
        in_specs=placed,
        out_specs=P(None, "blk", "cross", None, None, None),
        check_vma=False,
    )
```

```python
import functools
import math

import jax
import jax.numpy as jnp
from jax import lax
from jax.experimental import pallas as pl
from jax.experimental.pallas import tpu as pltpu
from jax.sharding import PartitionSpec as P

L = 256
STEPS = 2
F32 = jnp.float32
BF16 = jnp.bfloat16
VMEM = pl.BlockSpec(memory_space=pltpu.VMEM)
VMEM_BYTES = 40 << 20
SMALL_VMEM_BYTES = 8 << 20


def passed_along(value, axis, steps):
    count = lax.axis_size(axis)
    pairs = [(source, (source + steps) % count) for source in range(count)]
    return lax.ppermute(value, axis, pairs)


def lag_tables(bins, lags):
    bin_index = jnp.arange(bins, dtype=jnp.int32)
    odd_index = 2 * jnp.arange(lags // 2, dtype=jnp.int32) + 1
    phase_turns = jnp.mod(bin_index[:, None] * odd_index[None, :], 4 * bins).astype(F32)
    phase_angle = phase_turns * (math.pi / (2 * bins))
    cos_table = (jnp.cos(phase_angle) / bins).astype(BF16)
    sin_table = (-jnp.sin(phase_angle) / bins).astype(BF16)
    return (cos_table, sin_table)


def prepare_kernel(order_ref, quality_ref, raw_ref, out_ref):
    slots, _, bins = raw_ref.shape

    def eight(step, _):
        base = pl.multiple_of(step * 8, 8)
        real, imag, kept = [], [], []
        for i in range(8):
            channel = order_ref[0, base + i]
            pair = raw_ref[channel]
            real.append(pair[0:1, :])
            imag.append(pair[1:2, :])
            kept.append(jnp.full((1, 1), quality_ref[channel].astype(F32), F32))
        real = jnp.concatenate(real, axis=0)
        imag = jnp.concatenate(imag, axis=0)
        kept = jnp.concatenate(kept, axis=0)
        power = jnp.sum(real * real + imag * imag, axis=1, keepdims=True) / (2 * bins)
        scale = lax.rsqrt(power + 1e-06)
        out_ref[0, pl.ds(base, 8), :] = real * scale * kept
        out_ref[1, pl.ds(base, 8), :] = imag * scale * kept
        return 0

    lax.fori_loop(0, slots // 8, eight, 0)


def prepare(raw, quality, slot_order):
    slots, _, bins = raw.shape
    return pl.pallas_call(
        prepare_kernel,
        out_shape=jax.ShapeDtypeStruct((2, slots, bins), F32),
        in_specs=[
            pl.BlockSpec(memory_space=pltpu.SMEM),
            pl.BlockSpec(memory_space=pltpu.SMEM),
            VMEM,
        ],
        out_specs=VMEM,
        name="prepare",
        cost_estimate=pl.CostEstimate(flops=5 * raw.size, bytes_accessed=8 * raw.size, transcendentals=0),
    )(slot_order, quality, raw)


def select_kernel(owners_ref, shares_ref, own_ref, raw_ref, white_ref, read_sems, write_sems):
    steps = own_ref.shape[0]
    reads = [pltpu.make_async_copy(shares_ref.at[owners_ref[s, 0]], raw_ref.at[s], read_sems.at[s]) for s in range(steps)]
    writes = [pltpu.make_async_copy(white_ref.at[s], own_ref.at[s], write_sems.at[s]) for s in range(steps)]
    for read in reads:
        read.start()
    for s in range(steps):
        reads[s].wait()
        raw = raw_ref[s]
        count = 2 * raw.shape[2]
        power = jnp.sum(jnp.sum(raw * raw, axis=2, keepdims=True), axis=1, keepdims=True) / count
        white_ref[s] = raw * lax.rsqrt(power + 1e-06)
        writes[s].start()
    for write in writes:
        write.wait()


def select(shares, owners):
    own = (owners.shape[0],) + shares.shape[1:]
    return pl.pallas_call(
        select_kernel,
        out_shape=jax.ShapeDtypeStruct(own, F32),
        in_specs=[pl.BlockSpec(memory_space=pltpu.SMEM), pl.BlockSpec(memory_space=pl.ANY)],
        out_specs=pl.BlockSpec(memory_space=pl.ANY),
        scratch_shapes=[
            pltpu.VMEM(own, F32),
            pltpu.VMEM(own, F32),
            pltpu.SemaphoreType.DMA(own[:1]),
            pltpu.SemaphoreType.DMA(own[:1]),
        ],
        compiler_params=pltpu.CompilerParams(vmem_limit_bytes=SMALL_VMEM_BYTES),
        name="select",
    )(owners, shares)


def correlate_kernel(arrays, aliased, together, columns, where_ref, *refs):
    panel_refs, (slab_ref, table_ref) = refs[:arrays], refs[arrays : arrays + 2]
    out_ref, shares_ref, sems = refs[arrays + 2 + aliased :]
    width = shares_ref.shape[1]
    slots, bins = slab_ref.shape[1:]
    group = math.gcd(width, 8)
    step = pl.program_id(0)

    @pl.when(step == 0)
    def _():
        slot = 0
        for panel_ref in panel_refs:
            for row in range(panel_ref.shape[0]):
                pltpu.make_async_copy(panel_ref.at[row], shares_ref.at[slot], sems.at[slot]).start()
                slot += 1

    for i in range(together):
        slot = step * together + i
        pltpu.make_async_copy(panel_refs[0].at[0], shares_ref.at[slot], sems.at[slot]).wait()
    slab_re, slab_im = slab_ref[0], slab_ref[1]
    for i in range(together):
        share_ref = shares_ref.at[step * together + lax.rem(lax.div(where_ref[0], columns) + i, together)]
        for first in range(0, width, group):
            rows = []
            for p in range(first, first + group):
                pair = share_ref[p]
                re, im = pair[0:1, :], pair[1:2, :]
                inphase = (re * slab_re + im * slab_im).astype(BF16)
                quadrature = (im * slab_re - re * slab_im).astype(BF16)
                rows.append(jnp.concatenate([inphase, quadrature], axis=1))
            sums = jnp.dot(jnp.concatenate(rows, axis=0), table_ref[...], preferred_element_type=F32)
            for p in range(group):
                out_ref[i, first + p] = sums[p * slots : (p + 1) * slots].astype(BF16)


def correlate(out, step, panels, where, first, slab, table, columns, shifts, half=None):
    width, _, bins = panels[0].shape[1:]
    slots = slab.shape[1]
    lags = table.shape[1]
    arrays = len(panels)
    count = sum(panel.shape[0] for panel in panels)
    together = 2 if half is None else 1
    aliased = out is not None
    anywhere = pl.BlockSpec(memory_space=pl.ANY)

    def block(i, where):
        row = 0 if half is None else lax.rem(lax.div(where[0], columns) + half, 2)
        shift = sum(((i + first == a).astype(jnp.int32) * d for a, d in enumerate(shifts) if d), 0)
        return (step, row, lax.rem(where[0] + (columns - shift), columns), 0, 0, 0)

    grid_spec = pltpu.PrefetchScalarGridSpec(
        num_scalar_prefetch=1,
        grid=(count // together,),
        in_specs=[anywhere] * arrays + [VMEM, VMEM] + [anywhere] * aliased,
        out_specs=pl.BlockSpec((None, together, None, width, slots, lags), block),
        scratch_shapes=[pltpu.VMEM((count, width, 2, bins), F32), pltpu.SemaphoreType.DMA((count,))],
    )
    return pl.pallas_call(
        functools.partial(correlate_kernel, arrays, int(aliased), together, columns),
        out_shape=jax.ShapeDtypeStruct((STEPS, 2, columns, width, slots, lags), BF16),
        grid_spec=grid_spec,
        input_output_aliases={arrays + 3: 0} if aliased else {},
        compiler_params=pltpu.CompilerParams(vmem_limit_bytes=VMEM_BYTES),
        name="correlate",
        cost_estimate=pl.CostEstimate(
            flops=count * width * slots * bins * 4 * lags,
            bytes_accessed=count * width * slots * lags * 2 + 8 * slots * bins,
            transcendentals=0,
        ),
    )(where, *panels, slab, table, *([out] if aliased else []))


def local(receiver_spectra, source_spectra, quality, slot_order, owners):
    sources, _, bins = source_spectra.shape
    members = lax.axis_size("cross")
    width = sources // members
    row = members // 2
    me = lax.axis_index("cross")
    shifts = [0, 1, row - 1] + list(range(2, row - 1))
    where = me.astype(jnp.int32).reshape(1)
    mine = lax.dynamic_slice_in_dim(owners, lax.axis_index("blk"), 1, 1)

    shares = lax.all_to_all(source_spectra.reshape(members, width, 2, bins), "cross", 0, 0)
    cos_table, sin_table = lag_tables(bins, L)
    table = jnp.concatenate(
        [jnp.concatenate([cos_table, cos_table], axis=1), jnp.concatenate([sin_table, -sin_table], axis=1)], axis=0
    )
    slab0 = prepare(receiver_spectra, quality, slot_order)
    shares, slab0, table, where, mine = lax.optimization_barrier((shares, slab0, table, where, mine))

    own = select(shares, mine)
    across = [(i, (i + row) % members) for i in range(members)]
    rings = [[(i, i // row * row + (i + d) % row) for i in range(members)] for d in shifts[1:]]

    other0 = lax.ppermute(own[:1], "cross", across)
    pair0 = jnp.concatenate([own[:1], other0], axis=0)
    pair0, own1 = lax.optimization_barrier((pair0, own[1:]))
    rest0 = [lax.ppermute(pair0, "cross", ring) for ring in rings]
    other1 = lax.ppermute(own1, "cross", across)
    other1, sent = lax.optimization_barrier((other1, slab0))
    slab1 = passed_along(sent, "blk", 1)
    pair1 = jnp.concatenate([own[1:], other1], axis=0)

    out = correlate(None, 0, [own[:1]], where, 0, slab0, table, row, shifts, half=0)
    out = correlate(out, 0, [other0], where, 0, slab0, table, row, shifts, half=1)
    rest1 = [lax.ppermute(pair1, "cross", ring) for ring in rings]
    out = correlate(out, 0, rest0, where, 1, slab0, table, row, shifts)
    out = correlate(out, 1, [pair1] + rest1, where, 0, slab1, table, row, shifts)
    slots, lags = out.shape[-2:]
    return out.reshape(STEPS, 1, 1, sources, slots, lags)


def solution(mesh):
    placed = (
        P(("blk", "cross"), None, None),
        P(("blk", "cross"), None, None),
        P(("blk", "cross")),
        P(("blk", "cross"), None),
        P(),
    )
    return jax.shard_map(
        local,
        mesh=mesh,
        in_specs=placed,
        out_specs=P(None, "blk", "cross", None, None, None),
        check_vma=False,
    )
```
